32 devices in a mesh: ctx: 16 (over z, x, core), tp: 2 (over y).
Axes of the slice: x: 2, y: 2, z: 4, core: 2. Of those that a mesh axis runs over, the one named last changes fastest.
Arguments:
- queries: bfloat16 [4096, 8192], P('ctx', 'tp'), may hold values from -8 to 8
- key_rows: bfloat16 [4096, 1024], P('ctx', 'tp'), may hold values from -8 to 8
- value_head_rows: bfloat16 [4096, 1024], P('ctx', 'tp'), may hold values from -6 to 6
- ssm_input: bfloat16 [4096, 8192], P('ctx', 'tp'), may hold values from -6 to 6
- gate_input: bfloat16 [4096, 8192], P('ctx', 'tp'), may hold values from -6 to 6
- b_matrix: bfloat16 [4096, 1024], P('ctx', 'tp'), may hold values from -6 to 6
- c_matrix: bfloat16 [4096, 1024], P('ctx', 'tp'), may hold values from -0.5 to 0.5
- step_size: float32 [128, 4096], P('tp', 'ctx'), may hold values from 0.02 to 0.2
- log_decay: float32 [128, 4096], P('tp', 'ctx'), may hold values from -1.5 to 0
- skip_gain: float32 [128], P('tp'), may hold values from 0.5 to 1.5
- norm_gain: bfloat16 [8192], P('tp'), may hold values from 0.099609375 to 1.8984375
Outputs:
- attention_out: bfloat16 [4096, 8192], P('ctx', 'tp')
- mixer_out: bfloat16 [4096, 8192], P('ctx', 'tp')
The draws below stay inside these ranges and needn't reach their ends.
All inputs are finite; a program needn't handle non-finite values.
Results may differ from the reference program's by a relative error of at most 0.022.
Values may be sent and summed in bfloat16 or wider, within the bound.
A program may use at most 128 MiB of HBM per device.

```python
import math
import jax
import jax.numpy as jnp
from jax import lax

QUERY_HEADS = 64
KEY_VALUE_HEADS = 8
HEAD_WIDTH = 128
STATE_HEADS = 128
P_SIZE = 64
N = 128
GROUPS = 8
TOK_DEV = 256
SEQUENCE_TOKENS = 4096
INNER = 8192
N_CTX = 16


def draw_queries(key, part):
    sender_index = jax.random.fold_in(key, 11)
    sampled_values = 2.0 * jax.random.truncated_normal(sender_index, -4.0, 4.0, (SEQUENCE_TOKENS, QUERY_HEADS * HEAD_WIDTH), jnp.float32)
    return sampled_values.astype(jnp.bfloat16)


def draw_key_rows(key, part):
    sender_index = jax.random.fold_in(key, 13)
    sampled_values = jax.random.truncated_normal(sender_index, -6.0, 6.0, (SEQUENCE_TOKENS, KEY_VALUE_HEADS * HEAD_WIDTH), jnp.float32)
    return sampled_values.astype(jnp.bfloat16)


def draw_log_decay(key, part):
    random_subkeys = [jax.random.fold_in(key, 31 + offset) for offset in range(7)]
    slow_share = 0.5
    is_slow = jax.random.bernoulli(random_subkeys[0], slow_share, (STATE_HEADS, 1))
    slow_rate = jnp.exp(jax.random.uniform(random_subkeys[1], (STATE_HEADS, 1), jnp.float32, math.log(0.1), math.log(0.35))) / SEQUENCE_TOKENS
    fast_rate = jnp.exp(jax.random.uniform(random_subkeys[2], (STATE_HEADS, 1), jnp.float32, math.log(0.004), math.log(0.033)))
    per_block = jnp.exp(jax.random.uniform(random_subkeys[3], (STATE_HEADS, SEQUENCE_TOKENS // TOK_DEV), jnp.float32, math.log(0.5), math.log(2.0)))
    per_block = jnp.repeat(per_block, TOK_DEV, axis=1)
    roughness = jnp.exp(jax.random.uniform(random_subkeys[4], (STATE_HEADS, SEQUENCE_TOKENS), jnp.float32, math.log(0.6), math.log(1.6)))
    spike_start = jax.random.randint(random_subkeys[5], (STATE_HEADS, 2, 1), 0, SEQUENCE_TOKENS)
    spike_length = jax.random.uniform(random_subkeys[6], (STATE_HEADS, 2, 1), jnp.float32, 0.22, 0.69)
    token_index = jnp.arange(SEQUENCE_TOKENS)[None, None, :]
    spike_list = jnp.sum(jnp.where(token_index == spike_start, spike_length, 0.0), axis=1)
    decay_speed = jnp.where(is_slow, slow_rate, fast_rate) * per_block * roughness
    return -(decay_speed + spike_list)


def level_of(rng, dims, split, smallest, largest):
    gain, own = 1.0, jax.random.fold_in(rng, 6)
    for dim, shards_of in split:
        heights = jnp.exp(jax.random.uniform(jax.random.fold_in(own, dim), (shards_of,), jnp.float32, smallest / len(split), largest / len(split)))
        gain = gain * jnp.repeat(heights, dims[dim] // shards_of).reshape([-1 if axis == dim else 1 for axis in range(len(dims))])
    return gain


def noise(own_key, dims, scale, bound, shards=(), kind=jnp.bfloat16):
    array = jax.random.normal(own_key, dims, jnp.float32) * scale
    if len(shards) > 0:
        array = level_of(own_key, dims, shards, -0.22, 0.18) * array
    return jnp.clip(array, min=-bound, max=bound).astype(kind)


def setup_inputs(seed: int = 0) -> dict:
    seeds = jax.random.split(jax.random.key(seed), 12)
    queries = draw_queries(jax.random.fold_in(seeds[11], 71), 0)
    key_rows = draw_key_rows(jax.random.fold_in(seeds[11], 71), 0)
    value_head_rows = noise(seeds[2], (SEQUENCE_TOKENS, KEY_VALUE_HEADS * HEAD_WIDTH), 1.0, 6.0, ((0, 16), (1, 2)))
    ssm_input = noise(seeds[3], (SEQUENCE_TOKENS, INNER), 1.0, 6.0, ((0, 16), (1, 2)))
    gate_input = noise(seeds[4], (SEQUENCE_TOKENS, INNER), 1.0, 6.0, ((0, 16), (1, 2)))
    b_matrix = noise(seeds[5], (SEQUENCE_TOKENS, GROUPS * N), 1.0, 6.0, ((0, 16), (1, 2)))
    c_matrix = noise(seeds[6], (SEQUENCE_TOKENS, GROUPS * N), N ** -0.5, 0.5, ((0, 16), (1, 2)))
    step_size = jnp.clip(jnp.exp(math.log(0.2) - 2.3025851 * jax.random.uniform(seeds[7], (STATE_HEADS, SEQUENCE_TOKENS), jnp.float32) ** level_of(seeds[7], (STATE_HEADS, SEQUENCE_TOKENS), ((0, 2), (1, 16)), -0.2, 0.2)), 0.02, 0.2)
    log_decay = draw_log_decay(jax.random.fold_in(seeds[11], 71), 0)
    skip_gain = jnp.clip(0.5 + 1.0 * jax.random.uniform(seeds[9], (STATE_HEADS,), jnp.float32) ** level_of(seeds[9], (STATE_HEADS,), ((0, 2),), -0.2, 0.2), 0.5, 1.5)
    norm_gain = jnp.clip(1.0 + 0.18 * jax.random.normal(seeds[10], (INNER,), jnp.float32), 0.099609375, 1.8984375).astype(jnp.bfloat16)
    return {"queries": queries, "key_rows": key_rows, "value_head_rows": value_head_rows, "ssm_input": ssm_input, "gate_input": gate_input, "b_matrix": b_matrix, "c_matrix": c_matrix, "step_size": step_size, "log_decay": log_decay, "skip_gain": skip_gain, "norm_gain": norm_gain}


causal_score = -1e+30

def attention_part(queries, key_rows, value_head_rows):
    block_length = min(512, SEQUENCE_TOKENS)
    block_total = SEQUENCE_TOKENS // block_length
    query_per_key_heads = QUERY_HEADS // KEY_VALUE_HEADS
    score_factor = HEAD_WIDTH ** (-0.5)

    def query_block(block_id):
        q_start = block_id * block_length
        query_head_rows = lax.dynamic_slice_in_dim(queries, q_start, block_length, 0).astype(jnp.float32)
        query_head_rows = query_head_rows.reshape(block_length, KEY_VALUE_HEADS, query_per_key_heads, HEAD_WIDTH)
        query_pos = q_start + jnp.arange(block_length, dtype=jnp.int32)

        def key_step(key_block_id, running):
            run_max, run_sum, summed_so_far = running
            k_start = key_block_id * block_length
            key_portion = lax.dynamic_slice_in_dim(key_rows, k_start, block_length, 0).astype(jnp.float32)
            key_portion = key_portion.reshape(block_length, KEY_VALUE_HEADS, HEAD_WIDTH)
            value_portion = lax.dynamic_slice_in_dim(value_head_rows, k_start, block_length, 0).astype(jnp.float32)
            value_portion = value_portion.reshape(block_length, KEY_VALUE_HEADS, HEAD_WIDTH)
            key_pos = k_start + jnp.arange(block_length, dtype=jnp.int32)
            is_valid = key_pos[None, :] <= query_pos[:, None]
            score_matrix = jnp.einsum('faqo,bao->aqfb', query_head_rows, key_portion) * score_factor
            score_matrix = jnp.where(is_valid, score_matrix, causal_score)
            new_max = jnp.maximum(run_max, lax.optimization_barrier(jnp.max(score_matrix, axis=-1)))
            weights = jnp.where(is_valid, jnp.exp(score_matrix - new_max[..., None]), 0.0)
            correction_factor = jnp.exp(run_max - new_max)
            run_sum = run_sum * correction_factor + lax.optimization_barrier(jnp.sum(weights, axis=-1))
            quantized_values = lax.optimization_barrier(weights.astype(jnp.bfloat16)).astype(jnp.float32)
            summed_so_far = summed_so_far * correction_factor[..., None] + jnp.einsum('wlhc,cwm->wlhm', quantized_values, value_portion)
            return (new_max, run_sum, summed_so_far)
        starting_state = (jnp.full((KEY_VALUE_HEADS, query_per_key_heads, block_length), causal_score, jnp.float32), jnp.zeros((KEY_VALUE_HEADS, query_per_key_heads, block_length), jnp.float32), jnp.zeros((KEY_VALUE_HEADS, query_per_key_heads, block_length, HEAD_WIDTH), jnp.float32))
        run_max, run_sum, summed_so_far = lax.fori_loop(0, block_id + 1, key_step, starting_state)
        result = summed_so_far / run_sum[..., None]
        return result.transpose(2, 0, 1, 3).reshape(block_length, QUERY_HEADS * HEAD_WIDTH).astype(jnp.bfloat16)
    blocks_out = lax.map(query_block, jnp.arange(block_total, dtype=jnp.int32))
    return blocks_out.reshape(SEQUENCE_TOKENS, QUERY_HEADS * HEAD_WIDTH)

def mixer_part(ssm_input, gate_input, b_matrix, c_matrix, step_size, log_decay, skip_gain, norm_gain):
    heads_group = STATE_HEADS // GROUPS
    causal = jnp.tril(jnp.ones((TOK_DEV, TOK_DEV), dtype=bool))

    def ssm_block(carried, block_id):
        b_start = block_id * TOK_DEV
        mixer_in = lax.dynamic_slice_in_dim(ssm_input, b_start, TOK_DEV, 0).reshape(TOK_DEV, GROUPS, heads_group, P_SIZE)
        in_maps = lax.dynamic_slice_in_dim(b_matrix, b_start, TOK_DEV, 0).reshape(TOK_DEV, GROUPS, N)
        out_maps = lax.dynamic_slice_in_dim(c_matrix, b_start, TOK_DEV, 0).reshape(TOK_DEV, GROUPS, N)
        steps_here = lax.dynamic_slice_in_dim(step_size, b_start, TOK_DEV, 1).reshape(GROUPS, heads_group, TOK_DEV)
        decay_here = lax.dynamic_slice_in_dim(log_decay, b_start, TOK_DEV, 1).reshape(GROUPS, heads_group, TOK_DEV)
        cumul = jnp.cumsum(decay_here, axis=-1)
        mixer_f = mixer_in.astype(jnp.float32)
        out_f = out_maps.astype(jnp.float32)
        gram = jnp.einsum('tgn,sgn->gts', out_f, in_maps.astype(jnp.float32))
        spread = jnp.where(causal, cumul[..., :, None] - cumul[..., None, :], 0.0)
        mixing = jnp.where(causal, gram[:, None] * jnp.exp(spread) * steps_here[..., None, :], 0.0)
        mixing = lax.optimization_barrier(mixing.astype(jnp.bfloat16)).astype(jnp.float32)
        inner = jnp.einsum('ghts,sghp->tghp', mixing, mixer_f)
        carried_out = jnp.einsum('ghpn,tgn->tghp', carried, out_f, precision=lax.Precision.HIGHEST)
        carried_out = carried_out * jnp.exp(cumul).transpose(2, 0, 1)[..., None]
        direct = skip_gain.reshape(GROUPS, heads_group)[None, :, :, None] * mixer_f
        outputs = inner + carried_out + direct
        weight_end = jnp.exp(cumul[..., -1:] - cumul) * steps_here
        weighted = (mixer_f * weight_end.transpose(2, 0, 1)[..., None]).astype(jnp.bfloat16)
        weighted = lax.optimization_barrier(weighted).astype(jnp.float32)
        local_state = jnp.einsum('sghp,sgn->ghpn', weighted, in_maps.astype(jnp.float32))
        new_state = jnp.exp(cumul[..., -1])[..., None, None] * carried + local_state
        return (new_state, outputs.reshape(TOK_DEV, INNER))
    start_state = jnp.zeros((GROUPS, heads_group, P_SIZE, N), jnp.float32)
    _, mixed = lax.scan(ssm_block, start_state, jnp.arange(N_CTX, dtype=jnp.int32))
    mixed = mixed.reshape(SEQUENCE_TOKENS, INNER)
    gated = mixed * jax.nn.silu(gate_input.astype(jnp.float32))
    mean_square = lax.optimization_barrier(jnp.mean(gated * gated, axis=-1, keepdims=True))
    return (gated * lax.rsqrt(mean_square + 1e-05) * norm_gain.astype(jnp.float32)).astype(jnp.bfloat16)

def reference(queries, key_rows, value_head_rows, ssm_input, gate_input, b_matrix, c_matrix, step_size, log_decay, skip_gain, norm_gain):
    attention_out = attention_part(queries, key_rows, value_head_rows)
    mixer_out = mixer_part(ssm_input, gate_input, b_matrix, c_matrix, step_size, log_decay, skip_gain, norm_gain)
    return (attention_out, mixer_out)
```

```python
import functools
import math

import jax
import jax.numpy as jnp
from jax import lax
from jax.experimental import pallas as pl
from jax.experimental.pallas import tpu as pltpu
from jax.sharding import PartitionSpec as P

HEAD_WIDTH = 128
STATE_HEADS = 128
P_SIZE = 64
N = 128
CHUNK = 1024
HEADS_STEP = 4
VMEM_LIMIT = 48 * 1024 * 1024

causal_score = -1e30


def passed_along(block, axis, distance):
    devices = range(lax.axis_size(axis))
    route = [(i - distance, i) for i in devices if i - distance in devices]
    return lax.ppermute(block, axis, route)


def swapped(block, axis):
    return lax.ppermute(block, axis, [(i, i ^ 1) for i in range(lax.axis_size(axis))])


def attend_kernel(chunk, *refs):
    kv_ref, q_ref = refs[:2]
    o_ref, m_scr, acc_scr = refs[-3:]
    rows = q_ref.shape[0]
    heads = q_ref.shape[1] // HEAD_WIDTH
    factor = HEAD_WIDTH ** (-0.5) * math.log2(math.e)
    q_start = lax.axis_index("ctx") * rows
    last = q_start // chunk

    def sweep(c, first):
        start = pl.multiple_of(c * chunk, chunk)
        keys = kv_ref[pl.ds(start, chunk), :HEAD_WIDTH]
        values = kv_ref[pl.ds(start, chunk), HEAD_WIDTH:]
        values = jnp.concatenate([values, jnp.ones_like(values)], axis=1)
        if first:
            gap = lax.broadcasted_iota(jnp.int32, (rows, chunk), 0) - lax.broadcasted_iota(
                jnp.int32, (rows, chunk), 1
            )
            valid = gap >= start - q_start

        @pl.loop(0, heads // HEADS_STEP)
        def _(outer):
            for inner in range(HEADS_STEP):
                h = outer * HEADS_STEP + inner
                q = q_ref[:, pl.ds(pl.multiple_of(h * HEAD_WIDTH, HEAD_WIDTH), HEAD_WIDTH)]
                s = lax.dot_general(
                    q, keys, (((1,), (1,)), ((), ())), preferred_element_type=jnp.float32
                )
                if first:
                    s = jnp.where(valid, s, causal_score)
                top = jnp.max(s, axis=1, keepdims=True)
                if first:
                    p = jnp.exp2((s - top) * factor)
                    acc_scr[h] = jnp.dot(
                        p.astype(jnp.bfloat16), values, preferred_element_type=jnp.float32
                    )
                    m_scr[h] = jnp.broadcast_to(top, (rows, HEAD_WIDTH))
                else:
                    old = m_scr[h]
                    new = jnp.maximum(old, top)
                    p = jnp.exp2((s - new[:, :1]) * factor)
                    r = jnp.dot(p.astype(jnp.bfloat16), values, preferred_element_type=jnp.float32)
                    a = jnp.exp2((old - new) * factor)
                    acc_scr[h, :, :HEAD_WIDTH] = acc_scr[h, :, :HEAD_WIDTH] * a + r[:, :HEAD_WIDTH]
                    acc_scr[h, :, HEAD_WIDTH:] = acc_scr[h, :, HEAD_WIDTH:] * a + r[:, HEAD_WIDTH:]
                    m_scr[h] = new

    sweep(last, True)

    @pl.loop(0, last)
    def _(c):
        sweep(c, False)

    for h in range(heads):
        o_ref[:, h * HEAD_WIDTH : (h + 1) * HEAD_WIDTH] = (
            acc_scr[h, :, :HEAD_WIDTH] / acc_scr[h, :, HEAD_WIDTH:]
        ).astype(o_ref.dtype)


def attend(kv, queries, so_far, head, kv_heads):
    rows, width = queries.shape
    cols = width // kv_heads
    keys = kv.shape[0]
    chunk = CHUNK if keys % CHUNK == 0 and CHUNK % rows == 0 else rows
    q_heads = cols // HEAD_WIDTH
    in_specs = [
        pl.BlockSpec((keys, 2 * HEAD_WIDTH), lambda i: (0, 0)),
        pl.BlockSpec((rows, cols), lambda i: (0, head)),
    ]
    operands = [kv, queries]
    aliases = {}
    if so_far is not None:
        in_specs.append(pl.BlockSpec(memory_space=pl.ANY))
        operands.append(so_far)
        aliases = {2: 0}
    return pl.pallas_call(
        functools.partial(attend_kernel, chunk),
        grid=(1,),
        out_shape=jax.ShapeDtypeStruct((rows, width), jnp.bfloat16),
        in_specs=in_specs,
        out_specs=pl.BlockSpec((rows, cols), lambda i: (0, head)),
        scratch_shapes=[
            pltpu.VMEM((q_heads, rows, HEAD_WIDTH), jnp.float32),
            pltpu.VMEM((q_heads, rows, 2 * HEAD_WIDTH), jnp.float32),
        ],
        input_output_aliases=aliases,
        compiler_params=pltpu.CompilerParams(vmem_limit_bytes=VMEM_LIMIT),
        cost_estimate=pl.CostEstimate(
            flops=8 * rows * keys * cols, bytes_accessed=4 * keys * HEAD_WIDTH, transcendentals=0
        ),
        name="attend",
    )(*operands)


def pair_select(rows, first, second):
    lane = lax.broadcasted_iota(jnp.int32, (rows, 2 * P_SIZE), 1)
    return jnp.where(lane < P_SIZE, first, second)


def state_kernel(x_ref, b_ref, w_ref, s_ref):
    rows = x_ref.shape[0]
    maps = b_ref[...]
    for pair in range(x_ref.shape[1] // (2 * P_SIZE)):
        lanes = slice(pair * 2 * P_SIZE, (pair + 1) * 2 * P_SIZE)
        scale = pair_select(
            rows, w_ref[0, :, 2 * pair : 2 * pair + 1], w_ref[0, :, 2 * pair + 1 : 2 * pair + 2]
        )
        weighted = (x_ref[:, lanes].astype(jnp.float32) * scale).astype(jnp.bfloat16)
        s_ref[lanes, :] = lax.dot_general(
            weighted, maps, (((0,), (0,)), ((), ())), preferred_element_type=jnp.float32
        )


def inner_kernel(x_ref, b_ref, c_ref, ccol_ref, crow_ref, step_ref, skip_ref, y_ref):
    rows = x_ref.shape[0]
    gram = lax.dot_general(
        c_ref[...], b_ref[...], (((1,), (1,)), ((), ())), preferred_element_type=jnp.float32
    )
    causal = lax.broadcasted_iota(jnp.int32, (rows, rows), 0) >= lax.broadcasted_iota(
        jnp.int32, (rows, rows), 1
    )
    gram = jnp.where(causal, gram, 0.0)
    for pair in range(x_ref.shape[1] // (2 * P_SIZE)):
        lanes = slice(pair * 2 * P_SIZE, (pair + 1) * 2 * P_SIZE)
        x = x_ref[:, lanes]
        parts = []
        for h in (2 * pair, 2 * pair + 1):
            spread = jnp.minimum(ccol_ref[0, :, h : h + 1] - crow_ref[0, h : h + 1, :], 0.0)
            mixing = gram * jnp.exp(spread) * step_ref[0, h : h + 1, :]
            parts.append(
                jnp.dot(mixing.astype(jnp.bfloat16), x, preferred_element_type=jnp.float32)
            )
        direct = skip_ref[:, lanes] * x.astype(jnp.float32)
        y_ref[:, lanes] = pair_select(rows, parts[0], parts[1]) + direct


def gate_kernel(y_ref, s_ref, c_ref, e_ref, gate_ref, g_ref, sq_ref):
    rows = y_ref.shape[0]
    carried = lax.dot_general(
        c_ref[...], s_ref[...], (((1,), (1,)), ((), ())), preferred_element_type=jnp.float32
    )
    total = jnp.zeros((rows, 2 * P_SIZE), jnp.float32)
    for pair in range(y_ref.shape[1] // (2 * P_SIZE)):
        lanes = slice(pair * 2 * P_SIZE, (pair + 1) * 2 * P_SIZE)
        grow = pair_select(
            rows, e_ref[0, :, 2 * pair : 2 * pair + 1], e_ref[0, :, 2 * pair + 1 : 2 * pair + 2]
        )
        out = y_ref[:, lanes] + carried[:, lanes] * grow
        v = gate_ref[:, lanes].astype(jnp.float32)
        gated = out * (v / (1.0 + jnp.exp(-v)))
        g_ref[:, lanes] = gated
        total += gated * gated
    square = jnp.sum(total, axis=1, keepdims=True)

    @pl.when(pl.program_id(0) == 0)
    def _():
        sq_ref[...] = square

    @pl.when(pl.program_id(0) > 0)
    def _():
        sq_ref[...] += square


def norm_kernel(count, g_ref, sq_ref, gain_ref, o_ref):
    scaling = lax.rsqrt(sq_ref[...] / count + 1e-05)
    o_ref[...] = (g_ref[...] * scaling * gain_ref[...].astype(jnp.float32)).astype(o_ref.dtype)


def incoming_state(local_state, ends):
    count = lax.axis_size("ctx")
    position = lax.axis_index("ctx")
    heads = local_state.shape[0]
    half = heads // 2
    core = position % 2
    pair = position // 2
    pairs = count // 2
    all_ends = lax.all_gather(ends, "ctx")
    low = core == 0
    bf = jnp.bfloat16

    sent = jnp.where(low, local_state[half:], local_state[:half]).astype(bf)
    mine = jnp.where(low, local_state[:half], local_state[half:])
    theirs = swapped(sent, "ctx").astype(jnp.float32)
    ends_half = jnp.where(low, all_ends[:, :half], all_ends[:, half:])
    pair_ends = ends_half.reshape(pairs, 2, half)
    first = jnp.where(low, mine, theirs)
    second = jnp.where(low, theirs, mine)
    own = lax.dynamic_index_in_dim(pair_ends, pair, 0, keepdims=False)
    pair_logs = pair_ends[:, 0] + pair_ends[:, 1]
    index = jnp.arange(pairs)[:, None]

    def window(last, width):
        inside = (index > last - width) & (index <= last)
        return jnp.exp(jnp.sum(jnp.where(inside, pair_logs, 0.0), axis=0))[:, None, None]

    total = jnp.exp(own[1])[:, None, None] * first + second
    width = 1
    while 2 * width < pairs:
        before = passed_along(total.astype(bf), "ctx", 2 * width).astype(jnp.float32)
        total = total + window(pair, width) * before
        width *= 2
    packed = total.astype(bf)
    near = passed_along(packed, "ctx", 2).astype(jnp.float32)
    far = passed_along(packed, "ctx", 2 * (1 + width)).astype(jnp.float32)
    enter = near + window(pair - 1, width) * far
    enter_second = jnp.exp(own[0])[:, None, None] * enter + first
    for_me = jnp.where(low, enter, enter_second).astype(bf)
    for_them = jnp.where(low, enter_second, enter).astype(bf)
    got = swapped(for_them, "ctx")
    return jnp.where(
        low, jnp.concatenate([for_me, got], axis=0), jnp.concatenate([got, for_me], axis=0)
    )


def local(
    queries,
    key_rows,
    value_head_rows,
    ssm_input,
    gate_input,
    b_matrix,
    c_matrix,
    step_size,
    log_decay,
    skip_gain,
    norm_gain,
):
    rows = queries.shape[0]
    kv_heads = key_rows.shape[1] // HEAD_WIDTH
    gathered = []
    for g in range(kv_heads):
        cols = slice(g * HEAD_WIDTH, (g + 1) * HEAD_WIDTH)
        both = jnp.concatenate([key_rows[:, cols], value_head_rows[:, cols]], axis=1)
        gathered.append(lax.all_gather(both, "ctx", axis=0, tiled=True))

    heads = step_size.shape[0]
    groups = b_matrix.shape[1] // N
    per = heads // groups
    width = per * P_SIZE
    until = jnp.triu(jnp.ones((rows, rows), jnp.float32))
    cumul = jnp.dot(log_decay, until, precision=lax.Precision.HIGHEST)
    ends = cumul[:, -1]
    weight_end = jnp.exp(ends[:, None] - cumul) * step_size

    def by_group(a):
        return a.reshape(groups, per, rows)

    def columns(a):
        return by_group(a).transpose(0, 2, 1)

    params = pltpu.CompilerParams(vmem_limit_bytes=VMEM_LIMIT)
    wide = pl.BlockSpec((rows, width), lambda g: (0, g))
    narrow = pl.BlockSpec((rows, N), lambda g: (0, g))
    column = pl.BlockSpec((1, rows, per), lambda g: (g, 0, 0))
    row = pl.BlockSpec((1, per, rows), lambda g: (g, 0, 0))
    line = pl.BlockSpec((1, width), lambda g: (0, g))
    state = pl.BlockSpec((width, N), lambda g: (g, 0))

    local_state = pl.pallas_call(
        state_kernel,
        grid=(groups,),
        in_specs=[wide, narrow, column],
        out_specs=state,
        out_shape=jax.ShapeDtypeStruct((groups * width, N), jnp.float32),
        compiler_params=params,
        cost_estimate=pl.CostEstimate(
            flops=8 * rows * heads * P_SIZE * N, bytes_accessed=4 << 20, transcendentals=0
        ),
        name="local_state",
    )(ssm_input, b_matrix, columns(weight_end))

    entering = incoming_state(local_state.reshape(heads, P_SIZE, N), ends)

    inner = pl.pallas_call(
        inner_kernel,
        grid=(groups,),
        in_specs=[wide, narrow, narrow, column, row, row, line],
        out_specs=wide,
        out_shape=jax.ShapeDtypeStruct((rows, groups * width), jnp.float32),
        compiler_params=params,
        cost_estimate=pl.CostEstimate(
            flops=40 * rows * rows * heads * P_SIZE, bytes_accessed=6 << 20, transcendentals=0
        ),
        name="inner",
    )(
        ssm_input,
        b_matrix,
        c_matrix,
        columns(cumul),
        by_group(cumul),
        by_group(step_size),
        jnp.repeat(skip_gain, P_SIZE)[None, :],
    )

    attention_out = None
    for g in range(kv_heads):
        attention_out = attend(gathered[g], queries, attention_out, g, kv_heads)

    gated, square = pl.pallas_call(
        gate_kernel,
        grid=(groups,),
        in_specs=[wide, state, narrow, column, wide],
        out_specs=[wide, pl.BlockSpec((rows, 1), lambda g: (0, 0))],
        out_shape=[
            jax.ShapeDtypeStruct((rows, groups * width), jnp.float32),
            jax.ShapeDtypeStruct((rows, 1), jnp.float32),
        ],
        compiler_params=params,
        cost_estimate=pl.CostEstimate(
            flops=16 * rows * heads * P_SIZE * N, bytes_accessed=11 << 20, transcendentals=0
        ),
        name="gated",
    )(inner, entering.reshape(groups * width, N), c_matrix, columns(jnp.exp(cumul)), gate_input)
    square = lax.psum(square, "tp")
    mixer_out = pl.pallas_call(
        functools.partial(norm_kernel, STATE_HEADS * P_SIZE),
        grid=(groups,),
        in_specs=[wide, pl.BlockSpec((rows, 1), lambda g: (0, 0)), line],
        out_specs=wide,
        out_shape=jax.ShapeDtypeStruct((rows, groups * width), jnp.bfloat16),
        compiler_params=params,
        name="norm",
    )(gated, square, norm_gain[None, :])
    return (attention_out, mixer_out)


def solution(mesh):
    placed = (
        P("ctx", "tp"),
        P("ctx", "tp"),
        P("ctx", "tp"),
        P("ctx", "tp"),
        P("ctx", "tp"),
        P("ctx", "tp"),
        P("ctx", "tp"),
        P("tp", "ctx"),
        P("tp", "ctx"),
        P("tp"),
        P("tp"),
    )
    return jax.shard_map(
        local,
        mesh=mesh,
        in_specs=placed,
        out_specs=(P("ctx", "tp"), P("ctx", "tp")),
        check_vma=False,
    )
```

```python
import functools
import math

import jax
import jax.numpy as jnp
from jax import lax
from jax.experimental import pallas as pl
from jax.experimental.pallas import tpu as pltpu
from jax.sharding import PartitionSpec as P

HEAD_WIDTH = 128
STATE_HEADS = 128
P_SIZE = 64
N = 128
HEADS_STEP = 4
VMEM_LIMIT = 48 * 1024 * 1024

causal_score = -1e30


def passed_along(block, axis, distance):
    devices = range(lax.axis_size(axis))
    route = [(i - distance, i) for i in devices if i - distance in devices]
    return lax.ppermute(block, axis, route)


def swapped(block, axis):
    return lax.ppermute(block, axis, [(i, i ^ 1) for i in range(lax.axis_size(axis))])


ROW = 4


def attend_kernel(kv_ref, q_ref, o_ref, buf, m_scr, acc_scr, zs, zr, xs, xr, ps, pr, fs, fr):
    groups, rows = kv_ref.shape[:2]
    chunk = ROW * rows
    per = q_ref.shape[1] // HEAD_WIDTH // groups
    factor = HEAD_WIDTH ** (-0.5) * math.log2(math.e)
    me = lax.axis_index("ctx")
    lines = buf.shape[0]
    line = me // ROW
    place = me % ROW
    core = me % 2
    side = (me // 2) % 2
    mate = me + 1 - 2 * core
    across = me + 2 - 4 * side
    across_place = place + 2 - 4 * side
    steps = (line + 1) * groups

    def slot(age, g, at):
        return buf.at[age, g, pl.ds(pl.multiple_of(at * rows, rows), rows)]

    def send(src, dst, a, b, to):
        return pltpu.make_async_remote_copy(
            src_ref=src,
            dst_ref=dst,
            send_sem=a,
            recv_sem=b,
            device_id={"ctx": to},
            device_id_type=pl.DeviceIdType.MESH,
        )

    def down(age, g, to):
        return send(kv_ref.at[g], slot(age, g, place), zs.at[age, g], zr.at[age, g], to)

    def to_mate(age, g, src):
        return send(src, slot(age, g, place), ps.at[age, g], pr.at[age, g], mate)

    def to_across(age, g, src):
        return send(src, slot(age, g, place), xs.at[age, g], xr.at[age, g], across)

    def forward(age, g):
        here = slot(age, g, across_place)
        return send(here, here, fs.at[age, g], fr.at[age, g], mate)

    barrier = pltpu.get_barrier_semaphore()
    for d in range(1, lines):
        other = ((line + d) % lines) * ROW + place
        pl.semaphore_signal(
            barrier, inc=1, device_id={"ctx": other}, device_id_type=pl.DeviceIdType.MESH
        )
    for other in (mate, across):
        pl.semaphore_signal(
            barrier, inc=1, device_id={"ctx": other}, device_id_type=pl.DeviceIdType.MESH
        )
    pl.semaphore_wait(barrier, lines + 1)

    for g in range(groups):
        to_across(0, g, kv_ref.at[g]).start()
        to_mate(0, g, kv_ref.at[g]).start()
    for d in range(1, lines):

        @pl.when(line + d < lines)
        def _():
            for g in range(groups):
                down(d, g, me + d * ROW).start()

    for g in range(groups):
        buf[0, g, pl.ds(pl.multiple_of(place * rows, rows), rows), :] = kv_ref[g]

    def spread(t):
        age, g = t // groups, t % groups
        down(age, g, mate).wait_recv()
        to_across(age, g, slot(age, g, place)).start()
        to_mate(age, g, slot(age, g, place)).start()

    def relay(t):
        age, g = t // groups, t % groups
        to_across(age, g, slot(age, g, place)).wait_recv()
        forward(age, g).start()

    def work(age, g, first):
        keys = buf[age, g, :, :HEAD_WIDTH]
        values = buf[age, g, :, HEAD_WIDTH:]
        values = jnp.concatenate([values, jnp.ones_like(values)], axis=1)

        @pl.loop(0, per // HEADS_STEP)
        def _(outer):
            for inner in range(HEADS_STEP):
                h = g * per + outer * HEADS_STEP + inner
                q = q_ref[:, pl.ds(pl.multiple_of(h * HEAD_WIDTH, HEAD_WIDTH), HEAD_WIDTH)]
                s = lax.dot_general(
                    q, keys, (((1,), (1,)), ((), ())), preferred_element_type=jnp.float32
                )
                if first:
                    gap = lax.broadcasted_iota(jnp.int32, (rows, chunk), 0)
                    gap = gap - lax.broadcasted_iota(jnp.int32, (rows, chunk), 1)
                    s = jnp.where(gap >= -place * rows, s, causal_score)
                top = jnp.max(s, axis=1, keepdims=True)
                if first:
                    p = jnp.exp2((s - top) * factor)
                    acc_scr[h] = jnp.dot(
                        p.astype(jnp.bfloat16), values, preferred_element_type=jnp.float32
                    )
                    m_scr[h] = jnp.broadcast_to(top, (rows, HEAD_WIDTH))
                else:
                    old = m_scr[h]
                    new = jnp.maximum(old, top)
                    p = jnp.exp2((s - new[:, :1]) * factor)
                    r = jnp.dot(p.astype(jnp.bfloat16), values, preferred_element_type=jnp.float32)
                    a = jnp.exp2((old - new) * factor)
                    acc_scr[h, :, :HEAD_WIDTH] = acc_scr[h, :, :HEAD_WIDTH] * a + r[:, :HEAD_WIDTH]
                    acc_scr[h, :, HEAD_WIDTH:] = acc_scr[h, :, HEAD_WIDTH:] * a + r[:, HEAD_WIDTH:]
                    m_scr[h] = new

    for t in range(groups, 2):
        pl.when(t < steps)(functools.partial(spread, t))
    relay(0)

    @pl.loop(0, steps)
    def _(s):
        pl.when((s + 2 < steps) & (s + 2 >= groups))(lambda: spread(s + 2))
        pl.when(s + 1 < steps)(lambda: relay(s + 1))
        age, g = s // groups, s % groups
        to_mate(age, g, slot(age, g, place)).wait_recv()
        forward(age, g).wait_recv()
        pl.when(age == 0)(lambda: work(0, g, True))
        pl.when(age > 0)(lambda: work(age, g, False))

    @pl.loop(0, steps)
    def _(s):
        age, g = s // groups, s % groups
        to_across(age, g, slot(age, g, place)).wait_send()
        to_mate(age, g, slot(age, g, place)).wait_send()
        forward(age, g).wait_send()

    for d in range(1, lines):

        @pl.when(line + d < lines)
        def _():
            for g in range(groups):
                down(d, g, mate).wait_send()

    @pl.loop(0, per * groups)
    def _(h):
        o_ref[:, pl.ds(pl.multiple_of(h * HEAD_WIDTH, HEAD_WIDTH), HEAD_WIDTH)] = (
            acc_scr[h, :, :HEAD_WIDTH] / acc_scr[h, :, HEAD_WIDTH:]
        ).astype(o_ref.dtype)


def attend(kv, queries):
    groups, rows, both = kv.shape
    lines = lax.axis_size("ctx") // ROW
    heads = queries.shape[1] // HEAD_WIDTH
    vmem = pl.BlockSpec(memory_space=pltpu.VMEM)
    sems = pltpu.SemaphoreType.DMA((lines, groups))
    return pl.pallas_call(
        attend_kernel,
        out_shape=jax.ShapeDtypeStruct(queries.shape, jnp.bfloat16),
        in_specs=[vmem, vmem],
        out_specs=vmem,
        scratch_shapes=[
            pltpu.VMEM((lines, groups, ROW * rows, both), jnp.bfloat16),
            pltpu.VMEM((heads, rows, HEAD_WIDTH), jnp.float32),
            pltpu.VMEM((heads, rows, 2 * HEAD_WIDTH), jnp.float32),
        ]
        + [sems] * 8,
        compiler_params=pltpu.CompilerParams(
            vmem_limit_bytes=VMEM_LIMIT, collective_id=0, has_side_effects=True
        ),
        cost_estimate=pl.CostEstimate(
            flops=40 * rows * rows * heads * HEAD_WIDTH * lines,
            bytes_accessed=8 << 20,
            transcendentals=0,
        ),
        name="attend",
    )(kv, queries)


def pair_select(rows, first, second):
    lane = lax.broadcasted_iota(jnp.int32, (rows, 2 * P_SIZE), 1)
    return jnp.where(lane < P_SIZE, first, second)


def state_kernel(x_ref, b_ref, w_ref, s_ref):
    rows = x_ref.shape[0]
    maps = b_ref[...]
    for pair in range(x_ref.shape[1] // (2 * P_SIZE)):
        lanes = slice(pair * 2 * P_SIZE, (pair + 1) * 2 * P_SIZE)
        scale = pair_select(
            rows, w_ref[0, :, 2 * pair : 2 * pair + 1], w_ref[0, :, 2 * pair + 1 : 2 * pair + 2]
        )
        weighted = (x_ref[:, lanes].astype(jnp.float32) * scale).astype(jnp.bfloat16)
        s_ref[lanes, :] = lax.dot_general(
            weighted, maps, (((0,), (0,)), ((), ())), preferred_element_type=jnp.float32
        )


def inner_kernel(x_ref, b_ref, c_ref, ccol_ref, crow_ref, step_ref, skip_ref, y_ref):
    rows = x_ref.shape[0]
    gram = lax.dot_general(
        c_ref[...], b_ref[...], (((1,), (1,)), ((), ())), preferred_element_type=jnp.float32
    )
    causal = lax.broadcasted_iota(jnp.int32, (rows, rows), 0) >= lax.broadcasted_iota(
        jnp.int32, (rows, rows), 1
    )
    gram = jnp.where(causal, gram, 0.0)
    for pair in range(x_ref.shape[1] // (2 * P_SIZE)):
        lanes = slice(pair * 2 * P_SIZE, (pair + 1) * 2 * P_SIZE)
        x = x_ref[:, lanes]
        parts = []
        for h in (2 * pair, 2 * pair + 1):
            spread = jnp.minimum(ccol_ref[0, :, h : h + 1] - crow_ref[0, h : h + 1, :], 0.0)
            mixing = gram * jnp.exp(spread) * step_ref[0, h : h + 1, :]
            parts.append(
                jnp.dot(mixing.astype(jnp.bfloat16), x, preferred_element_type=jnp.float32)
            )
        direct = skip_ref[:, lanes] * x.astype(jnp.float32)
        y_ref[:, lanes] = pair_select(rows, parts[0], parts[1]) + direct


def gate_kernel(y_ref, s_ref, c_ref, e_ref, gate_ref, g_ref, sq_ref):
    rows = y_ref.shape[0]
    carried = lax.dot_general(
        c_ref[...], s_ref[...], (((1,), (1,)), ((), ())), preferred_element_type=jnp.float32
    )
    total = jnp.zeros((rows, 2 * P_SIZE), jnp.float32)
    for pair in range(y_ref.shape[1] // (2 * P_SIZE)):
        lanes = slice(pair * 2 * P_SIZE, (pair + 1) * 2 * P_SIZE)
        grow = pair_select(
            rows, e_ref[0, :, 2 * pair : 2 * pair + 1], e_ref[0, :, 2 * pair + 1 : 2 * pair + 2]
        )
        out = y_ref[:, lanes] + carried[:, lanes] * grow
        v = gate_ref[:, lanes].astype(jnp.float32)
        gated = out * (v / (1.0 + jnp.exp(-v)))
        g_ref[:, lanes] = gated
        total += gated * gated
    square = jnp.sum(total, axis=1, keepdims=True)

    @pl.when(pl.program_id(0) == 0)
    def _():
        sq_ref[...] = square

    @pl.when(pl.program_id(0) > 0)
    def _():
        sq_ref[...] += square


def norm_kernel(count, g_ref, sq_ref, gain_ref, o_ref):
    scaling = lax.rsqrt(sq_ref[...] / count + 1e-05)
    o_ref[...] = (g_ref[...] * scaling * gain_ref[...].astype(jnp.float32)).astype(o_ref.dtype)


def incoming_state(local_state, ends):
    count = lax.axis_size("ctx")
    position = lax.axis_index("ctx")
    heads = local_state.shape[0]
    half = heads // 2
    core = position % 2
    pair = position // 2
    pairs = count // 2
    all_ends = lax.all_gather(ends, "ctx")
    low = core == 0
    bf = jnp.bfloat16

    sent = jnp.where(low, local_state[half:], local_state[:half]).astype(bf)
    mine = jnp.where(low, local_state[:half], local_state[half:])
    theirs = swapped(sent, "ctx").astype(jnp.float32)
    ends_half = jnp.where(low, all_ends[:, :half], all_ends[:, half:])
    pair_ends = ends_half.reshape(pairs, 2, half)
    first = jnp.where(low, mine, theirs)
    second = jnp.where(low, theirs, mine)
    own = lax.dynamic_index_in_dim(pair_ends, pair, 0, keepdims=False)
    pair_logs = pair_ends[:, 0] + pair_ends[:, 1]
    index = jnp.arange(pairs)[:, None]

    def window(last, width):
        inside = (index > last - width) & (index <= last)
        return jnp.exp(jnp.sum(jnp.where(inside, pair_logs, 0.0), axis=0))[:, None, None]

    total = jnp.exp(own[1])[:, None, None] * first + second
    width = 1
    while 2 * width < pairs:
        before = passed_along(total.astype(bf), "ctx", 2 * width).astype(jnp.float32)
        total = total + window(pair, width) * before
        width *= 2
    packed = total.astype(bf)
    near = passed_along(packed, "ctx", 2).astype(jnp.float32)
    far = passed_along(packed, "ctx", 2 * (1 + width)).astype(jnp.float32)
    enter = near + window(pair - 1, width) * far
    enter_second = jnp.exp(own[0])[:, None, None] * enter + first
    for_me = jnp.where(low, enter, enter_second).astype(bf)
    for_them = jnp.where(low, enter_second, enter).astype(bf)
    got = swapped(for_them, "ctx")
    return jnp.where(
        low, jnp.concatenate([for_me, got], axis=0), jnp.concatenate([got, for_me], axis=0)
    )


def local(
    queries,
    key_rows,
    value_head_rows,
    ssm_input,
    gate_input,
    b_matrix,
    c_matrix,
    step_size,
    log_decay,
    skip_gain,
    norm_gain,
):
    rows = queries.shape[0]
    kv_heads = key_rows.shape[1] // HEAD_WIDTH
    kv = jnp.stack([key_rows, value_head_rows], axis=1)
    kv = kv.reshape(rows, 2, kv_heads, HEAD_WIDTH).transpose(2, 0, 1, 3)
    kv = kv.reshape(kv_heads, rows, 2 * HEAD_WIDTH)

    heads = step_size.shape[0]
    groups = b_matrix.shape[1] // N
    per = heads // groups
    width = per * P_SIZE
    until = jnp.triu(jnp.ones((rows, rows), jnp.float32))
    cumul = jnp.dot(log_decay, until, precision=lax.Precision.HIGHEST)
    ends = cumul[:, -1]
    weight_end = jnp.exp(ends[:, None] - cumul) * step_size

    def by_group(a):
        return a.reshape(groups, per, rows)

    def columns(a):
        return by_group(a).transpose(0, 2, 1)

    params = pltpu.CompilerParams(vmem_limit_bytes=VMEM_LIMIT)
    wide = pl.BlockSpec((rows, width), lambda g: (0, g))
    narrow = pl.BlockSpec((rows, N), lambda g: (0, g))
    column = pl.BlockSpec((1, rows, per), lambda g: (g, 0, 0))
    row = pl.BlockSpec((1, per, rows), lambda g: (g, 0, 0))
    line = pl.BlockSpec((1, width), lambda g: (0, g))
    state = pl.BlockSpec((width, N), lambda g: (g, 0))

    local_state = pl.pallas_call(
        state_kernel,
        grid=(groups,),
        in_specs=[wide, narrow, column],
        out_specs=state,
        out_shape=jax.ShapeDtypeStruct((groups * width, N), jnp.float32),
        compiler_params=params,
        cost_estimate=pl.CostEstimate(
            flops=8 * rows * heads * P_SIZE * N, bytes_accessed=4 << 20, transcendentals=0
        ),
        name="local_state",
    )(ssm_input, b_matrix, columns(weight_end))

    entering = incoming_state(local_state.reshape(heads, P_SIZE, N), ends)

    inner = pl.pallas_call(
        inner_kernel,
        grid=(groups,),
        in_specs=[wide, narrow, narrow, column, row, row, line],
        out_specs=wide,
        out_shape=jax.ShapeDtypeStruct((rows, groups * width), jnp.float32),
        compiler_params=params,
        cost_estimate=pl.CostEstimate(
            flops=40 * rows * rows * heads * P_SIZE, bytes_accessed=6 << 20, transcendentals=0
        ),
        name="inner",
    )(
        ssm_input,
        b_matrix,
        c_matrix,
        columns(cumul),
        by_group(cumul),
        by_group(step_size),
        jnp.repeat(skip_gain, P_SIZE)[None, :],
    )

    attention_out = attend(kv, queries)

    gated, square = pl.pallas_call(
        gate_kernel,
        grid=(groups,),
        in_specs=[wide, state, narrow, column, wide],
        out_specs=[wide, pl.BlockSpec((rows, 1), lambda g: (0, 0))],
        out_shape=[
            jax.ShapeDtypeStruct((rows, groups * width), jnp.float32),
            jax.ShapeDtypeStruct((rows, 1), jnp.float32),
        ],
        compiler_params=params,
        cost_estimate=pl.CostEstimate(
            flops=16 * rows * heads * P_SIZE * N, bytes_accessed=11 << 20, transcendentals=0
        ),
        name="gated",
    )(inner, entering.reshape(groups * width, N), c_matrix, columns(jnp.exp(cumul)), gate_input)
    square = lax.psum(square, "tp")
    mixer_out = pl.pallas_call(
        functools.partial(norm_kernel, STATE_HEADS * P_SIZE),
        grid=(groups,),
        in_specs=[wide, pl.BlockSpec((rows, 1), lambda g: (0, 0)), line],
        out_specs=wide,
        out_shape=jax.ShapeDtypeStruct((rows, groups * width), jnp.bfloat16),
        compiler_params=params,
        name="norm",
    )(gated, square, norm_gain[None, :])
    return (attention_out, mixer_out)


def solution(mesh):
    placed = (
        P("ctx", "tp"),
        P("ctx", "tp"),
        P("ctx", "tp"),
        P("ctx", "tp"),
        P("ctx", "tp"),
        P("ctx", "tp"),
        P("ctx", "tp"),
        P("tp", "ctx"),
        P("tp", "ctx"),
        P("tp"),
        P("tp"),
    )
    return jax.shard_map(
        local,
        mesh=mesh,
        in_specs=placed,
        out_specs=(P("ctx", "tp"), P("ctx", "tp")),
        check_vma=False,
    )
```

```python
import functools
import math

import jax
import jax.numpy as jnp
from jax import lax
from jax.experimental import pallas as pl
from jax.experimental.pallas import tpu as pltpu
from jax.sharding import PartitionSpec as P

HEAD_WIDTH = 128
STATE_HEADS = 128
P_SIZE = 64
N = 128
HEADS_STEP = 4
VMEM_LIMIT = 48 * 1024 * 1024

causal_score = -1e30


ROW = 4


def attend_kernel(
    widths, kv_ref, q_ref, st_ref, dec_ref, o_ref, in_ref, buf, m_scr, acc_scr, zs, zr, xs, xr,
    ps, pr, fs, fr, out_buf, in_buf, dec_out, dec_in, total, lead, dec_tot, dec_lead, ss, sr, ds, dr
):
    groups, rows = kv_ref.shape[:2]
    chunk = ROW * rows
    per = q_ref.shape[1] // HEAD_WIDTH // groups
    factor = HEAD_WIDTH ** (-0.5) * math.log2(math.e)
    me = lax.axis_index("ctx")
    lines = buf.shape[0]
    line = me // ROW
    place = me % ROW
    core = me % 2
    side = (me // 2) % 2
    mate = me + 1 - 2 * core
    across = me + 2 - 4 * side
    across_place = place + 2 - 4 * side
    steps = (line + 1) * groups

    def slot(age, g, at):
        return buf.at[age, g, pl.ds(pl.multiple_of(at * rows, rows), rows)]

    def send(src, dst, a, b, to):
        return pltpu.make_async_remote_copy(
            src_ref=src,
            dst_ref=dst,
            send_sem=a,
            recv_sem=b,
            device_id={"ctx": to},
            device_id_type=pl.DeviceIdType.MESH,
        )

    def down(age, g, to):
        return send(kv_ref.at[g], slot(age, g, place), zs.at[age, g], zr.at[age, g], to)

    def to_mate(age, g, src):
        return send(src, slot(age, g, place), ps.at[age, g], pr.at[age, g], mate)

    def to_across(age, g, src):
        return send(src, slot(age, g, place), xs.at[age, g], xr.at[age, g], across)

    def forward(age, g):
        here = slot(age, g, across_place)
        return send(here, here, fs.at[age, g], fr.at[age, g], mate)

    barrier = pltpu.get_barrier_semaphore()
    for d in range(1, lines):
        other = ((line + d) % lines) * ROW + place
        pl.semaphore_signal(
            barrier, inc=1, device_id={"ctx": other}, device_id_type=pl.DeviceIdType.MESH
        )
    for other in (mate, across):
        pl.semaphore_signal(
            barrier, inc=1, device_id={"ctx": other}, device_id_type=pl.DeviceIdType.MESH
        )
    count = lines * ROW
    far = 1 + 2 * widths[-1] if widths else 2
    far_offset = 2 * far
    for other in (
        (me + 2) % count,
        (me + count - 2) % count,
        (me + far_offset) % count,
        (me + count - far_offset) % count,
    ):
        pl.semaphore_signal(
            barrier, inc=1, device_id={"ctx": other}, device_id_type=pl.DeviceIdType.MESH
        )
    pl.semaphore_wait(barrier, lines + 5)

    half = st_ref.shape[0] // 2
    pair = me // 2
    pairs = count // 2
    mine, other_half = core * half, (1 - core) * half
    near_slot = 1 + len(widths)
    far_slot, last_slot = near_slot + 1, near_slot + 2

    def state_copy(k, src_k, to):
        return send(out_buf.at[src_k], in_buf.at[k], ss.at[k], sr.at[k], to)

    def decay_copy(k, src_k, to):
        return send(dec_out.at[src_k], dec_in.at[k], ds.at[k], dr.at[k], to)

    def pass_on(k, distance):
        @pl.when(pair + distance < pairs)
        def _():
            state_copy(k, k, me + 2 * distance).start()
            decay_copy(k, k, me + 2 * distance).start()

    def pass_to_all(k):
        if k < near_slot:
            pass_on(k, widths[k - 1])
        else:
            pass_on(near_slot, 1)

            @pl.when(pair + far < pairs)
            def _():
                state_copy(far_slot, near_slot, me + far_offset).start()

    def begin_scan():
        @pl.loop(0, half)
        def _(h):
            out_buf[0, h] = st_ref[other_half + h].astype(jnp.bfloat16)
            dec_out[0, h] = dec_ref[other_half + h]

        state_copy(0, 0, mate).start()
        decay_copy(0, 0, mate).start()

    def pair_stage():
        state_copy(0, 0, mate).wait_recv()
        decay_copy(0, 0, mate).wait_recv()

        @pl.loop(0, half)
        def _(h):
            a, b = st_ref[mine + h], in_buf[0, h].astype(jnp.float32)
            da, db = dec_ref[mine + h], dec_in[0, h]
            low = core == 0
            first, second = jnp.where(low, a, b), jnp.where(low, b, a)
            d0, d1 = jnp.where(low, da, db), jnp.where(low, db, da)
            lead[h] = first
            dec_lead[h] = d0
            t = d1[:1] * first + second
            total[h] = t
            dec_tot[h] = d0 * d1
            out_buf[1, h] = t.astype(jnp.bfloat16)
            dec_out[1, h] = d0 * d1

        pass_to_all(1)

    def double_stage(k):
        @pl.when(pair >= widths[k - 1])
        def _():
            state_copy(k, k, mate).wait_recv()
            decay_copy(k, k, mate).wait_recv()

            @pl.loop(0, half)
            def _(h):
                d = dec_tot[h]
                total[h] = total[h] + d[:1] * in_buf[k, h].astype(jnp.float32)
                dec_tot[h] = d * dec_in[k, h]

        @pl.loop(0, half)
        def _(h):
            out_buf[k + 1, h] = total[h].astype(jnp.bfloat16)
            dec_out[k + 1, h] = dec_tot[h]

        pass_to_all(k + 1)

    def enter_stage():
        @pl.loop(0, half)
        def _(h):
            total[h] = jnp.zeros(total.shape[1:], jnp.float32)

        @pl.when(pair >= 1)
        def _():
            state_copy(near_slot, near_slot, mate).wait_recv()
            decay_copy(near_slot, near_slot, mate).wait_recv()

            @pl.loop(0, half)
            def _(h):
                total[h] = in_buf[near_slot, h].astype(jnp.float32)

        @pl.when(pair >= far)
        def _():
            state_copy(far_slot, near_slot, mate).wait_recv()

            @pl.loop(0, half)
            def _(h):
                total[h] = total[h] + dec_in[near_slot, h, :1] * in_buf[far_slot, h].astype(
                    jnp.float32
                )

        @pl.loop(0, half)
        def _(h):
            enter = total[h]
            second = dec_lead[h, :1] * enter + lead[h]
            low = core == 0
            in_ref[mine + h] = jnp.where(low, enter, second).astype(jnp.bfloat16)
            out_buf[last_slot, h] = jnp.where(low, second, enter).astype(jnp.bfloat16)

        state_copy(last_slot, last_slot, mate).start()

    def finish_stage():
        state_copy(last_slot, last_slot, mate).wait_recv()

        @pl.loop(0, half)
        def _(h):
            in_ref[other_half + h] = in_buf[last_slot, h]

    stages = [pair_stage]
    stages += [functools.partial(double_stage, k) for k in range(1, near_slot)]
    stages += [enter_stage, finish_stage]
    all_steps = lines * groups

    def finish_sends():
        for k in (0, last_slot):
            state_copy(k, k, mate).wait_send()
        decay_copy(0, 0, mate).wait_send()
        for k, distance in list(zip(range(1, near_slot), widths)) + [(near_slot, 1)]:

            @pl.when(pair + distance < pairs)
            def _():
                state_copy(k, k, mate).wait_send()
                decay_copy(k, k, mate).wait_send()

        @pl.when(pair + far < pairs)
        def _():
            state_copy(far_slot, near_slot, mate).wait_send()

    begin_scan()

    for g in range(groups):
        to_across(0, g, kv_ref.at[g]).start()
        to_mate(0, g, kv_ref.at[g]).start()
    for d in range(1, lines):

        @pl.when(line + d < lines)
        def _():
            for g in range(groups):
                down(d, g, me + d * ROW).start()

    for g in range(groups):
        buf[0, g, pl.ds(pl.multiple_of(place * rows, rows), rows), :] = kv_ref[g]

    def spread(t):
        age, g = t // groups, t % groups
        down(age, g, mate).wait_recv()
        to_across(age, g, slot(age, g, place)).start()
        to_mate(age, g, slot(age, g, place)).start()

    def relay(t):
        age, g = t // groups, t % groups
        to_across(age, g, slot(age, g, place)).wait_recv()
        forward(age, g).start()

    def work(age, g, first):
        keys = buf[age, g, :, :HEAD_WIDTH]
        values = buf[age, g, :, HEAD_WIDTH:]
        values = jnp.concatenate([values, jnp.ones_like(values)], axis=1)

        @pl.loop(0, per // HEADS_STEP)
        def _(outer):
            for inner in range(HEADS_STEP):
                h = g * per + outer * HEADS_STEP + inner
                q = q_ref[:, pl.ds(pl.multiple_of(h * HEAD_WIDTH, HEAD_WIDTH), HEAD_WIDTH)]
                s = lax.dot_general(
                    q, keys, (((1,), (1,)), ((), ())), preferred_element_type=jnp.float32
                )
                if first:
                    gap = lax.broadcasted_iota(jnp.int32, (rows, chunk), 0)
                    gap = gap - lax.broadcasted_iota(jnp.int32, (rows, chunk), 1)
                    s = jnp.where(gap >= -place * rows, s, causal_score)
                top = jnp.max(s, axis=1, keepdims=True)
                if first:
                    p = jnp.exp2((s - top) * factor)
                    acc_scr[h] = jnp.dot(
                        p.astype(jnp.bfloat16), values, preferred_element_type=jnp.float32
                    )
                    m_scr[h] = jnp.broadcast_to(top, (rows, HEAD_WIDTH))
                else:
                    old = m_scr[h]
                    new = jnp.maximum(old, top)
                    p = jnp.exp2((s - new[:, :1]) * factor)
                    r = jnp.dot(p.astype(jnp.bfloat16), values, preferred_element_type=jnp.float32)
                    a = jnp.exp2((old - new) * factor)
                    acc_scr[h, :, :HEAD_WIDTH] = acc_scr[h, :, :HEAD_WIDTH] * a + r[:, :HEAD_WIDTH]
                    acc_scr[h, :, HEAD_WIDTH:] = acc_scr[h, :, HEAD_WIDTH:] * a + r[:, HEAD_WIDTH:]
                    m_scr[h] = new

    for t in range(groups, 2):
        pl.when(t < steps)(functools.partial(spread, t))
    relay(0)

    def step(s):
        pl.when((s + 2 < steps) & (s + 2 >= groups))(lambda: spread(s + 2))
        pl.when(s + 1 < steps)(lambda: relay(s + 1))
        age, g = s // groups, s % groups
        to_mate(age, g, slot(age, g, place)).wait_recv()
        forward(age, g).wait_recv()
        pl.when(age == 0)(lambda: work(0, g, True))
        pl.when(age > 0)(lambda: work(age, g, False))

    @pl.loop(0, all_steps)
    def _(s):
        for k, stage in enumerate(stages):
            pl.when(s == (k + 1) * all_steps // (len(stages) + 1))(stage)
        pl.when(s < steps)(lambda: step(s))

    finish_sends()

    @pl.loop(0, steps)
    def _(s):
        age, g = s // groups, s % groups
        to_across(age, g, slot(age, g, place)).wait_send()
        to_mate(age, g, slot(age, g, place)).wait_send()
        forward(age, g).wait_send()

    for d in range(1, lines):

        @pl.when(line + d < lines)
        def _():
            for g in range(groups):
                down(d, g, mate).wait_send()

    @pl.loop(0, per * groups)
    def _(h):
        o_ref[:, pl.ds(pl.multiple_of(h * HEAD_WIDTH, HEAD_WIDTH), HEAD_WIDTH)] = (
            acc_scr[h, :, :HEAD_WIDTH] / acc_scr[h, :, HEAD_WIDTH:]
        ).astype(o_ref.dtype)


def attend(kv, queries, local_state, block_decay):
    groups, rows, both = kv.shape
    lines = lax.axis_size("ctx") // ROW
    heads = queries.shape[1] // HEAD_WIDTH
    pairs = lax.axis_size("ctx") // 2
    widths = [1 << k for k in range(pairs.bit_length()) if 2 << k < pairs]
    slots = len(widths) + 4
    shape = (local_state.shape[0] // 2,) + local_state.shape[1:]
    flat = (shape[0],) + block_decay.shape[1:]
    slot_sems = pltpu.SemaphoreType.DMA((slots,))
    vmem = pl.BlockSpec(memory_space=pltpu.VMEM)
    sems = pltpu.SemaphoreType.DMA((lines, groups))
    return pl.pallas_call(
        functools.partial(attend_kernel, widths),
        out_shape=[
            jax.ShapeDtypeStruct(queries.shape, jnp.bfloat16),
            jax.ShapeDtypeStruct(local_state.shape, jnp.bfloat16),
        ],
        in_specs=[vmem] * 4,
        out_specs=[vmem] * 2,
        scratch_shapes=[
            pltpu.VMEM((lines, groups, ROW * rows, both), jnp.bfloat16),
            pltpu.VMEM((heads, rows, HEAD_WIDTH), jnp.float32),
            pltpu.VMEM((heads, rows, 2 * HEAD_WIDTH), jnp.float32),
        ]
        + [sems] * 8
        + [
            pltpu.VMEM((slots,) + shape, jnp.bfloat16),
            pltpu.VMEM((slots,) + shape, jnp.bfloat16),
            pltpu.VMEM((slots,) + flat, jnp.float32),
            pltpu.VMEM((slots,) + flat, jnp.float32),
            pltpu.VMEM(shape, jnp.float32),
            pltpu.VMEM(shape, jnp.float32),
            pltpu.VMEM(flat, jnp.float32),
            pltpu.VMEM(flat, jnp.float32),
        ]
        + [slot_sems] * 4,
        compiler_params=pltpu.CompilerParams(
            vmem_limit_bytes=VMEM_LIMIT, collective_id=0, has_side_effects=True
        ),
        cost_estimate=pl.CostEstimate(
            flops=40 * rows * rows * heads * HEAD_WIDTH * lines,
            bytes_accessed=8 << 20,
            transcendentals=0,
        ),
        name="attend",
    )(kv, queries, local_state, block_decay)


def pair_select(rows, first, second):
    lane = lax.broadcasted_iota(jnp.int32, (rows, 2 * P_SIZE), 1)
    return jnp.where(lane < P_SIZE, first, second)


def state_kernel(x_ref, b_ref, w_ref, s_ref):
    rows = x_ref.shape[0]
    maps = b_ref[...]
    for pair in range(x_ref.shape[1] // (2 * P_SIZE)):
        lanes = slice(pair * 2 * P_SIZE, (pair + 1) * 2 * P_SIZE)
        scale = pair_select(
            rows, w_ref[0, :, 2 * pair : 2 * pair + 1], w_ref[0, :, 2 * pair + 1 : 2 * pair + 2]
        )
        weighted = (x_ref[:, lanes].astype(jnp.float32) * scale).astype(jnp.bfloat16)
        s_ref[lanes, :] = lax.dot_general(
            weighted, maps, (((0,), (0,)), ((), ())), preferred_element_type=jnp.float32
        )


def inner_kernel(x_ref, b_ref, c_ref, ccol_ref, crow_ref, step_ref, skip_ref, y_ref):
    rows = x_ref.shape[0]
    gram = lax.dot_general(
        c_ref[...], b_ref[...], (((1,), (1,)), ((), ())), preferred_element_type=jnp.float32
    )
    causal = lax.broadcasted_iota(jnp.int32, (rows, rows), 0) >= lax.broadcasted_iota(
        jnp.int32, (rows, rows), 1
    )
    gram = jnp.where(causal, gram, 0.0)
    for pair in range(x_ref.shape[1] // (2 * P_SIZE)):
        lanes = slice(pair * 2 * P_SIZE, (pair + 1) * 2 * P_SIZE)
        x = x_ref[:, lanes]
        parts = []
        for h in (2 * pair, 2 * pair + 1):
            spread = jnp.minimum(ccol_ref[0, :, h : h + 1] - crow_ref[0, h : h + 1, :], 0.0)
            mixing = gram * jnp.exp(spread) * step_ref[0, h : h + 1, :]
            parts.append(
                jnp.dot(mixing.astype(jnp.bfloat16), x, preferred_element_type=jnp.float32)
            )
        direct = skip_ref[:, lanes] * x.astype(jnp.float32)
        y_ref[:, lanes] = pair_select(rows, parts[0], parts[1]) + direct


def gate_kernel(y_ref, s_ref, c_ref, e_ref, gate_ref, g_ref, sq_ref):
    rows = y_ref.shape[0]
    carried = lax.dot_general(
        c_ref[...], s_ref[...], (((1,), (1,)), ((), ())), preferred_element_type=jnp.float32
    )
    total = jnp.zeros((rows, 2 * P_SIZE), jnp.float32)
    for pair in range(y_ref.shape[1] // (2 * P_SIZE)):
        lanes = slice(pair * 2 * P_SIZE, (pair + 1) * 2 * P_SIZE)
        grow = pair_select(
            rows, e_ref[0, :, 2 * pair : 2 * pair + 1], e_ref[0, :, 2 * pair + 1 : 2 * pair + 2]
        )
        out = y_ref[:, lanes] + carried[:, lanes] * grow
        v = gate_ref[:, lanes].astype(jnp.float32)
        gated = out * (v / (1.0 + jnp.exp(-v)))
        g_ref[:, lanes] = gated
        total += gated * gated
    square = jnp.sum(total, axis=1, keepdims=True)

    @pl.when(pl.program_id(0) == 0)
    def _():
        sq_ref[...] = square

    @pl.when(pl.program_id(0) > 0)
    def _():
        sq_ref[...] += square


def norm_kernel(count, g_ref, sq_ref, gain_ref, o_ref):
    scaling = lax.rsqrt(sq_ref[...] / count + 1e-05)
    o_ref[...] = (g_ref[...] * scaling * gain_ref[...].astype(jnp.float32)).astype(o_ref.dtype)


def local(
    queries,
    key_rows,
    value_head_rows,
    ssm_input,
    gate_input,
    b_matrix,
    c_matrix,
    step_size,
    log_decay,
    skip_gain,
    norm_gain,
):
    rows = queries.shape[0]
    kv_heads = key_rows.shape[1] // HEAD_WIDTH
    kv = jnp.stack([key_rows, value_head_rows], axis=1)
    kv = kv.reshape(rows, 2, kv_heads, HEAD_WIDTH).transpose(2, 0, 1, 3)
    kv = kv.reshape(kv_heads, rows, 2 * HEAD_WIDTH)

    heads = step_size.shape[0]
    groups = b_matrix.shape[1] // N
    per = heads // groups
    width = per * P_SIZE
    until = jnp.triu(jnp.ones((rows, rows), jnp.float32))
    cumul = jnp.dot(log_decay, until, precision=lax.Precision.HIGHEST)
    ends = cumul[:, -1]
    weight_end = jnp.exp(ends[:, None] - cumul) * step_size

    def by_group(a):
        return a.reshape(groups, per, rows)

    def columns(a):
        return by_group(a).transpose(0, 2, 1)

    params = pltpu.CompilerParams(vmem_limit_bytes=VMEM_LIMIT)
    wide = pl.BlockSpec((rows, width), lambda g: (0, g))
    narrow = pl.BlockSpec((rows, N), lambda g: (0, g))
    column = pl.BlockSpec((1, rows, per), lambda g: (g, 0, 0))
    row = pl.BlockSpec((1, per, rows), lambda g: (g, 0, 0))
    line = pl.BlockSpec((1, width), lambda g: (0, g))
    state = pl.BlockSpec((width, N), lambda g: (g, 0))

    local_state = pl.pallas_call(
        state_kernel,
        grid=(groups,),
        in_specs=[wide, narrow, column],
        out_specs=state,
        out_shape=jax.ShapeDtypeStruct((groups * width, N), jnp.float32),
        compiler_params=params,
        cost_estimate=pl.CostEstimate(
            flops=8 * rows * heads * P_SIZE * N, bytes_accessed=4 << 20, transcendentals=0
        ),
        name="local_state",
    )(ssm_input, b_matrix, columns(weight_end))

    block_decay = jnp.broadcast_to(jnp.exp(ends)[:, None, None], (heads, 8, N))
    attention_out, entering = attend(
        kv, queries, local_state.reshape(heads, P_SIZE, N), block_decay
    )

    inner = pl.pallas_call(
        inner_kernel,
        grid=(groups,),
        in_specs=[wide, narrow, narrow, column, row, row, line],
        out_specs=wide,
        out_shape=jax.ShapeDtypeStruct((rows, groups * width), jnp.float32),
        compiler_params=params,
        cost_estimate=pl.CostEstimate(
            flops=40 * rows * rows * heads * P_SIZE, bytes_accessed=6 << 20, transcendentals=0
        ),
        name="inner",
    )(
        ssm_input,
        b_matrix,
        c_matrix,
        columns(cumul),
        by_group(cumul),
        by_group(step_size),
        jnp.repeat(skip_gain, P_SIZE)[None, :],
    )

    gated, square = pl.pallas_call(
        gate_kernel,
        grid=(groups,),
        in_specs=[wide, state, narrow, column, wide],
        out_specs=[wide, pl.BlockSpec((rows, 1), lambda g: (0, 0))],
        out_shape=[
            jax.ShapeDtypeStruct((rows, groups * width), jnp.float32),
            jax.ShapeDtypeStruct((rows, 1), jnp.float32),
        ],
        compiler_params=params,
        cost_estimate=pl.CostEstimate(
            flops=16 * rows * heads * P_SIZE * N, bytes_accessed=11 << 20, transcendentals=0
        ),
        name="gated",
    )(inner, entering.reshape(groups * width, N), c_matrix, columns(jnp.exp(cumul)), gate_input)
    square = lax.psum(square, "tp")
    mixer_out = pl.pallas_call(
        functools.partial(norm_kernel, STATE_HEADS * P_SIZE),
        grid=(groups,),
        in_specs=[wide, pl.BlockSpec((rows, 1), lambda g: (0, 0)), line],
        out_specs=wide,
        out_shape=jax.ShapeDtypeStruct((rows, groups * width), jnp.bfloat16),
        compiler_params=params,
        name="norm",
    )(gated, square, norm_gain[None, :])
    return (attention_out, mixer_out)


def solution(mesh):
    placed = (
        P("ctx", "tp"),
        P("ctx", "tp"),
        P("ctx", "tp"),
        P("ctx", "tp"),
        P("ctx", "tp"),
        P("ctx", "tp"),
        P("ctx", "tp"),
        P("tp", "ctx"),
        P("tp", "ctx"),
        P("tp"),
        P("tp"),
    )
    return jax.shard_map(
        local,
        mesh=mesh,
        in_specs=placed,
        out_specs=(P("ctx", "tp"), P("ctx", "tp")),
        check_vma=False,
    )
```
